32 devices in a mesh: frame: 4 (over y, x), tile: 8 (over z, core).
Axes of the slice: x: 2, y: 2, z: 4, core: 2. Of those that a mesh axis runs over, the one named last changes fastest.
Arguments:
- point_feats: bfloat16 [4, 16, 81920], P('frame', None, 'tile'), may hold values from -6 to 6
- point_slot: int32 [4, 81920], P('frame', 'tile'), may hold values from 0 to 5119, as said below
- bucket_len: int32 [4, 64], P('frame', 'tile'), may hold values from 213 to 1280, as said below
- window_len: int32 [4, 320], P('frame', 'tile'), may hold values from 21 to 128, as said below
- w_vfe: bfloat16 [16, 128], replicated, may hold values from -1.5 to 1.5
- b_vfe: float32 [128], replicated, may hold values from -3 to 3
- gain_vfe: float32 [128], replicated, may hold values from 0.25 to 1.75
- w_qkv: bfloat16 [2, 128, 384], replicated, may hold values from -0.5 to 0.5
- b_qv: float32 [2, 256], replicated, may hold values from -2 to 2
- w_out: bfloat16 [2, 128, 128], replicated, may hold values from -1.5 to 1.5
- b_out: float32 [2, 128], replicated, may hold values from -2 to 2
- gain_attn: float32 [2, 128], replicated, may hold values from 0.25 to 1.75
- bias_attn: float32 [2, 128], replicated, may hold values from -2 to 2
- w_in: bfloat16 [2, 128, 256], replicated, may hold values from -0.5 to 0.5
- b_in: float32 [2, 256], replicated, may hold values from -3 to 3
- w_back: bfloat16 [2, 256, 128], replicated, may hold values from -0.375 to 0.375
- b_back: float32 [2, 128], replicated, may hold values from -2 to 2
- gain_ffn: float32 [2, 128], replicated, may hold values from 0.25 to 1.75
- bias_ffn: float32 [2, 128], replicated, may hold values from -2 to 2
- cotangent: bfloat16 [4, 40960, 128], P('frame', 'tile'), may hold values from -6 to 6
Outputs:
- pillar_out: bfloat16 [4, 40960, 128], P('frame', 'tile')
- grad_points: bfloat16 [4, 16, 81920], P('frame', None, 'tile')
- grad_w_vfe: float32 [16, 128], replicated
- grad_b_vfe: float32 [128], replicated
- grad_gain_vfe: float32 [128], replicated
- grad_w_qkv: float32 [2, 128, 384], replicated
- grad_b_qv: float32 [2, 256], replicated
- grad_w_out: float32 [2, 128, 128], replicated
- grad_b_out: float32 [2, 128], replicated
- grad_gain_attn: float32 [2, 128], replicated
- grad_bias_attn: float32 [2, 128], replicated
- grad_w_in: float32 [2, 128, 256], replicated
- grad_b_in: float32 [2, 256], replicated
- grad_w_back: float32 [2, 256, 128], replicated
- grad_b_back: float32 [2, 128], replicated
- grad_gain_ffn: float32 [2, 128], replicated
- grad_bias_ffn: float32 [2, 128], replicated
The draws below stay inside these ranges and needn't reach their ends.
Inputs may be any that keep to these rules, and one draw needn't show every extreme that they name: `point_slot`: every point names a slot of an occupied pillar of its owner tile: its position in its window is below that window's length. `bucket_len`: live points of a bucket fill its first slots; in every frame every source fills its bucket for the last tile. `window_len`: occupied pillars of a window fill its first slots; the last tile's last window is full.
All inputs are finite; a program needn't handle non-finite values.
Results may differ from the reference program's by a relative error of at most 0.019.
Values may be sent and summed in bfloat16 or wider, within the bound.
A program may use at most 192 MiB of HBM per device.

```python
import jax
import jax.numpy as jnp
from jax import lax

D = 128
HEADS = 8
FF = 256
PF = 16
WSLOT = 128
LAYERS = 2
NWIN = 40
PIL_DEV = 5120
TILES = 8
FRAMES = 4
PB = 1280
PILLARS = 40960
POINTS = 81920
WINDOWS = 320


def window_lengths(key):
    length_key = jax.random.fold_in(key, 101)
    full_key = jax.random.fold_in(key, 102)
    tile_index = jnp.arange(TILES, dtype=jnp.int32)
    ceiling = WSLOT * (TILES - 1 + 2 * tile_index) // (3 * max(TILES - 1, 1))
    ceiling = jnp.maximum(ceiling, 1)[None, :, None]
    lengths = jax.random.randint(length_key, (FRAMES, TILES, NWIN), (ceiling + 1) // 2, ceiling + 1, dtype=jnp.int32)
    chosen = jax.random.randint(full_key, (FRAMES, TILES, 1), 0, NWIN, dtype=jnp.int32)
    chosen = jnp.where(tile_index[None, :, None] == TILES - 1, NWIN - 1, chosen)
    window_index = jnp.arange(NWIN, dtype=jnp.int32)[None, None, :]
    lengths = jnp.where(window_index == chosen, ceiling, lengths)
    least_spot = (chosen + 1) % NWIN
    at_least = (tile_index[None, :, None] == 0) & (window_index == least_spot)
    lengths = jnp.where(at_least, (ceiling + 1) // 2, lengths)
    return lengths


def draw_window_len(key, part):
    lengths = window_lengths(key)
    return lengths.reshape(FRAMES, WINDOWS)


def draw_point_slot(key, part):
    lengths = window_lengths(key)
    key = jax.random.fold_in(key, 7)
    window_key, slot_key = jax.random.split(key)
    chosen = jax.random.randint(window_key, (FRAMES, TILES, TILES, PB), 0, NWIN, dtype=jnp.int32)
    spread_lengths = jnp.broadcast_to(lengths[:, None, :, :], (FRAMES, TILES, TILES, NWIN))
    owner_lengths = jnp.take_along_axis(spread_lengths, chosen, axis=3)
    slots = jax.random.randint(slot_key, chosen.shape, 0, owner_lengths, dtype=jnp.int32)
    rows = chosen * WSLOT + slots
    rows = rows.at[:, :, TILES - 1, 0].set(PIL_DEV - 1)
    rows = rows.at[:, :, TILES - 1, 1].set(0)
    return rows.reshape(FRAMES, POINTS)


def draw_bucket_len(key, part):
    key = jax.random.fold_in(key, 5)
    owner_index = jnp.arange(TILES, dtype=jnp.int32)
    ceiling = PB * (TILES - 1 + 2 * owner_index) // (3 * max(TILES - 1, 1))
    ceiling = ceiling[None, None, :]
    counts = jax.random.randint(key, (FRAMES, TILES, TILES), (ceiling + 1) // 2, ceiling + 1, dtype=jnp.int32)
    counts = jnp.where(owner_index[None, None, :] == TILES - 1, PB, counts)
    counts = counts.at[:, 0, 0].set((PB // 3 + 1) // 2)
    return counts.reshape(FRAMES, TILES * TILES)


def steps_of(key, shape, pieces, smallest, largest):
    gain, own = 1.0, jax.random.fold_in(key, 6)
    for axis_at, shards_of in pieces:
        draws = jnp.exp(jax.random.uniform(jax.random.fold_in(own, axis_at), (shards_of,), jnp.float32, smallest / len(pieces), largest / len(pieces)))
        gain = gain * jnp.repeat(draws, shape[axis_at] // shards_of).reshape([-1 if axis == axis_at else 1 for axis in range(len(shape))])
    return gain


def noise(own_key, extent, deviation, reach, cuts=(), kind=jnp.bfloat16):
    values = deviation * jax.random.normal(own_key, extent, jnp.float32)
    if cuts:
        values = values * steps_of(own_key, extent, cuts, -0.22, 0.18)
    return jnp.clip(values, -reach, reach).astype(kind)


def setup_inputs(seed: int = 0) -> dict:
    key_list = jax.random.split(jax.random.key(seed), 21)
    point_feats = noise(key_list[0], (FRAMES, PF, POINTS), 1.0, 6.0, ((0, 4), (2, 8)))
    point_slot = draw_point_slot(jax.random.fold_in(key_list[20], 71), 0)
    bucket_len = draw_bucket_len(jax.random.fold_in(key_list[20], 71), 0)
    window_len = draw_window_len(jax.random.fold_in(key_list[20], 71), 0)
    w_vfe = noise(key_list[4], (PF, D), PF ** -0.5, 1.5)
    b_vfe = noise(key_list[5], (D,), 0.5, 3.0, (), jnp.float32)
    gain_vfe = jnp.clip(1.0 + 0.15 * jax.random.normal(key_list[6], (D,), jnp.float32), 0.25, 1.75)
    w_qkv = noise(key_list[7], (LAYERS, D, 3 * D), D ** -0.5, 0.5)
    b_qv = noise(key_list[8], (LAYERS, 2 * D), 0.3, 2.0, (), jnp.float32)
    w_out = noise(key_list[9], (LAYERS, D, D), (D // 8) ** -0.5, 1.5)
    b_out = noise(key_list[10], (LAYERS, D), 0.3, 2.0, (), jnp.float32)
    gain_attn = jnp.clip(1.0 + 0.15 * jax.random.normal(key_list[11], (LAYERS, D), jnp.float32), 0.25, 1.75)
    bias_attn = noise(key_list[12], (LAYERS, D), 0.3, 2.0, (), jnp.float32)
    w_in = noise(key_list[13], (LAYERS, D, FF), D ** -0.5, 0.5)
    b_in = noise(key_list[14], (LAYERS, FF), 0.5, 3.0, (), jnp.float32)
    w_back = noise(key_list[15], (LAYERS, FF, D), FF ** -0.5, 0.375)
    b_back = noise(key_list[16], (LAYERS, D), 0.3, 2.0, (), jnp.float32)
    gain_ffn = jnp.clip(1.0 + 0.15 * jax.random.normal(key_list[17], (LAYERS, D), jnp.float32), 0.25, 1.75)
    bias_ffn = noise(key_list[18], (LAYERS, D), 0.3, 2.0, (), jnp.float32)
    cotangent = noise(key_list[19], (FRAMES, PILLARS, D), 1.0, 6.0, ((0, 4), (1, 8)))
    return dict(point_feats=point_feats, point_slot=point_slot, bucket_len=bucket_len, window_len=window_len, w_vfe=w_vfe, b_vfe=b_vfe, gain_vfe=gain_vfe, w_qkv=w_qkv, b_qv=b_qv, w_out=w_out, b_out=b_out, gain_attn=gain_attn, bias_attn=bias_attn, w_in=w_in, b_in=b_in, w_back=w_back, b_back=b_back, gain_ffn=gain_ffn, bias_ffn=bias_ffn, cotangent=cotangent)


@jax.custom_vjp
def low(v):
    return lax.optimization_barrier(v.astype(jnp.bfloat16)).astype(jnp.float32)

@jax.custom_vjp
def low_back(v):
    return v

def low_keep(v):
    return (low(v), None)

def low_pass(kept, grad):
    return (grad,)

def back_keep(v):
    return (v, None)

def back_low(kept, grad):
    return (low(grad),)
low.defvjp(low_keep, low_pass)
low_back.defvjp(back_keep, back_low)

def gelu_tanh(values):
    return jax.nn.gelu(values, approximate=True)

def matmul_high(left_side, right_side):
    return jnp.dot(left_side, right_side, precision=lax.Precision.HIGHEST)

def layer_norm(values, norm_gain, norm_bias):
    center = values - lax.optimization_barrier(jnp.mean(values, axis=-1, keepdims=True))
    spread = lax.optimization_barrier(jnp.mean(center * center, axis=-1, keepdims=True))
    return center * lax.rsqrt(spread + 1e-05) * norm_gain + norm_bias

def window_attend(queries, key_rows, val_rows, live_rows):
    window_count = queries.shape[0] // WSLOT
    head_dim = queries.shape[1] // HEADS
    grid_shape = (window_count, WSLOT, HEADS, head_dim)
    scores = jnp.einsum('wqhd,wkhd->whqk', queries.reshape(grid_shape), key_rows.reshape(grid_shape), precision=lax.Precision.HIGHEST) * head_dim ** (-0.5)
    scores = low_back(scores)
    allowed = live_rows.reshape(window_count, 1, 1, WSLOT) > 0.5
    masked = jnp.where(allowed, scores, -1e+30)
    row_peak = lax.optimization_barrier(jnp.max(masked, axis=-1, keepdims=True))
    denom_sum = lax.optimization_barrier(jnp.sum(jnp.exp(masked - row_peak), axis=-1, keepdims=True))
    weights_low = low(jnp.exp(masked - (row_peak + jnp.log(denom_sum))))
    mixture = jnp.einsum('whqk,wkhd->wqhd', weights_low, val_rows.reshape(grid_shape), precision=lax.Precision.HIGHEST)
    return mixture.reshape(queries.shape)

def encoder_layer(row_values, live_rows, params):
    w_qkv, b_qv, w_out, b_out, gain_attn, bias_attn, w_in, b_in, w_back, b_back, gain_ffn, bias_ffn = params
    model_width = row_values.shape[1]
    packed = matmul_high(low(row_values), w_qkv)
    queries = low(low_back(packed[:, :model_width] + b_qv[:model_width]))
    key_rows = low(low_back(packed[:, model_width:2 * model_width]))
    val_rows = low(low_back(packed[:, 2 * model_width:] + b_qv[model_width:]))
    mixture = low(low_back(window_attend(queries, key_rows, val_rows, live_rows)))
    branch = low_back(matmul_high(mixture, w_out) + b_out)
    normed = layer_norm(row_values + branch, gain_attn, bias_attn)
    inner_pre = low_back(matmul_high(low(normed), w_in) + b_in)
    outer_out = low_back(matmul_high(low(gelu_tanh(inner_pre)), w_back) + b_back)
    return layer_norm(normed + outer_out, gain_ffn, bias_ffn) * live_rows[:, None]

def run_layer(row_values, live_rows, params):

    def block_step(pair_inputs):
        return encoder_layer(pair_inputs[0], pair_inputs[1], params)
    blocks = lax.map(jax.checkpoint(block_step), (row_values.reshape(TILES, PIL_DEV, row_values.shape[1]), live_rows.reshape(TILES, PIL_DEV)))
    return blocks.reshape(row_values.shape)

def encode_points(frame_feats, point_rows, point_live, w_vfe, b_vfe):
    pre_act = low_back(matmul_high(frame_feats.T, w_vfe) + b_vfe)
    hidden = gelu_tanh(pre_act) * point_live[:, None]
    return low_back(jax.ops.segment_sum(hidden, point_rows, num_segments=PILLARS))

def frame_forward(frame_feats, point_rows, point_live, valid_rows, weights):
    w_vfe, b_vfe, gain_vfe, w_qkv, b_qv, w_out, b_out, gain_attn, bias_attn, w_in, b_in, w_back, b_back, gain_ffn, bias_ffn = weights
    pillar_sum = jax.checkpoint(encode_points)(frame_feats, point_rows, point_live, w_vfe, b_vfe)
    power_mean = lax.optimization_barrier(jnp.sum(valid_rows[:, None] * pillar_sum * pillar_sum, axis=0)) / jnp.sum(valid_rows)
    encoded = pillar_sum * lax.rsqrt(power_mean + 1e-05) * gain_vfe
    stacked = (w_qkv, b_qv, w_out, b_out, gain_attn, bias_attn, w_in, b_in, w_back, b_back, gain_ffn, bias_ffn)
    first_out = run_layer(encoded, valid_rows, tuple((weight[0] for weight in stacked)))
    half_slots = WSLOT // 2
    view_out = run_layer(jnp.roll(first_out, -half_slots, axis=0), jnp.roll(valid_rows, -half_slots), tuple((weight[1] for weight in stacked)))
    return jnp.roll(view_out, half_slots, axis=0)

def reference(point_feats, point_slot, bucket_len, window_len, w_vfe, b_vfe, gain_vfe, w_qkv, b_qv, w_out, b_out, gain_attn, bias_attn, w_in, b_in, w_back, b_back, gain_ffn, bias_ffn, cotangent):
    weights = tuple((weight.astype(jnp.float32) for weight in (w_vfe, b_vfe, gain_vfe, w_qkv, b_qv, w_out, b_out, gain_attn, bias_attn, w_in, b_in, w_back, b_back, gain_ffn, bias_ffn)))
    index_points = jnp.arange(POINTS, dtype=jnp.int32)
    owners = index_points // PB % TILES
    within = index_points % PB

    def one_frame(running, frame_inputs):
        frame_feats, frame_slots, buckets, lengths, cot_rows = frame_inputs
        point_rows = owners * PIL_DEV + frame_slots
        point_live = (within < buckets[index_points // PB]).astype(jnp.float32)
        valid_rows = (jnp.arange(WSLOT, dtype=jnp.int32)[None, :] < lengths[:, None]).reshape(PILLARS).astype(jnp.float32)

        def forward(feats_value, weight_set):
            return frame_forward(feats_value, point_rows, point_live, valid_rows, weight_set)
        result, pullback = jax.vjp(forward, frame_feats.astype(jnp.float32), weights)
        grad_feats, grad_weights = pullback(cot_rows.astype(jnp.float32))
        running = tuple((old_sum + new_term for old_sum, new_term in zip(running, grad_weights)))
        return (running, (result.astype(jnp.bfloat16), grad_feats.astype(jnp.bfloat16)))
    zero_sums = tuple((jnp.zeros_like(weight) for weight in weights))
    grad_sums, (outputs, grad_points) = lax.scan(one_frame, zero_sums, (point_feats, point_slot, bucket_len, window_len, cotangent))
    return (outputs, grad_points, grad_sums[0], grad_sums[1], grad_sums[2], grad_sums[3], grad_sums[4], grad_sums[5], grad_sums[6], grad_sums[7], grad_sums[8], grad_sums[9], grad_sums[10], grad_sums[11], grad_sums[12], grad_sums[13], grad_sums[14])
```

```python
import functools

import jax
import jax.numpy as jnp
from jax import lax
from jax.experimental import pallas as pl
from jax.experimental.pallas import tpu as pltpu
from jax.sharding import PartitionSpec as P

HEADS = 8
WSLOT = 128
D = 128
FF = 256
HD = D // HEADS
EPS = 1e-05
LOG2E = 1.4426950408889634
GC = 0.7978845608028654
GA = 0.044715
NACC = 8

f32 = jnp.float32
bf16 = jnp.bfloat16
VMEM = pl.BlockSpec(memory_space=pltpu.VMEM)
SMEM = pl.BlockSpec(memory_space=pltpu.SMEM)
VMEM_LIMIT = 56 * 1024 * 1024
MAIN_LIMIT = 62 * 1024 * 1024
GROUP = 10
LATENCY = 120


def dot(a, b):
    return lax.dot_general(a, b, (((1,), (0,)), ((), ())), preferred_element_type=f32)


def dot_nt(a, b):
    return lax.dot_general(a, b, (((1,), (1,)), ((), ())), preferred_element_type=f32)


def dot_tn(a, b):
    return lax.dot_general(a, b, (((0,), (0,)), ((), ())), preferred_element_type=f32)


PQ, PV, PO, PGA, PBA, PI0, PI1, PB, PGF, PBF = range(10)


def layer_scratch():
    return [
        pltpu.VMEM((3 * D, D), bf16),
        pltpu.VMEM((D, D), bf16),
        pltpu.VMEM((FF, D), bf16),
        pltpu.VMEM((D, FF), bf16),
        pltpu.VMEM((10, D, D), f32),
        pltpu.VMEM((HEADS // 2, WSLOT, D), bf16),
    ]


def prepare(layer, w, s):
    w_qkv, b_qv, w_out, b_out, g_at, b_at, w_in, b_in, w_back, b_back, g_ff, b_ff = w
    wqt, wot, wit, wbt, vec, cols = s
    for p in range(HEADS // 2):
        lane = lax.broadcasted_iota(jnp.int32, (WSLOT, D), 1)
        inside = (lane >= 2 * p * HD) & (lane < (2 * p + 2) * HD)
        cols[p] = inside.astype(f32).astype(bf16)
    wqt[0:D, :] = (w_qkv[layer, :, 0:D].astype(f32) * HD ** (-0.5)).T.astype(bf16)
    wqt[D:, :] = w_qkv[layer, :, D:].T
    wot[...] = w_out[layer].T
    wit[...] = w_in[layer].T
    wbt[...] = w_back[layer].T
    sl = slice(layer, layer + 1)
    rows = [
        b_qv[sl, 0:D], b_qv[sl, D : 2 * D], b_out[sl, :], g_at[sl, :], b_at[sl, :],
        b_in[sl, 0:D], b_in[sl, D : 2 * D], b_back[sl, :], g_ff[sl, :], b_ff[sl, :],
    ]
    for i, row in enumerate(rows):
        if i == PQ:
            row = row * HD ** (-0.5)
        vec[i] = jnp.broadcast_to(row, (D, D)).T


NPAIR = HEADS // 2
NQUAD = HEADS // 4
GROW = 64


def cat(xs):
    return jnp.concatenate(xs, axis=1)


def mean0(v):
    return jnp.sum(v, axis=0, keepdims=True) * (1.0 / D)


def norm0(v):
    c = v - mean0(v)
    rs = lax.rsqrt(mean0(c * c) + EPS)
    return c * rs, rs


def norm0_back(gy, xh, rs):
    return rs * (gy - mean0(gy) - xh * mean0(gy * xh))


def gelu(x):
    return x * (0.5 + 0.5 * jnp.tanh(x * (GC + (GC * GA) * (x * x))))


def gelu_low(x):
    u = x * x
    t = jnp.tanh((x * (GC + (GC * GA) * u)).astype(bf16))
    xb, ub = x.astype(bf16), u.astype(bf16)
    h = bf16(0.5) + bf16(0.5) * t
    act = xb * h
    grad = h + act * ((bf16(1.0) - h) * (bf16(2.0 * GC) + bf16(6.0 * GC * GA) * ub))
    return act, grad


def window_masks(shifted, lens, win):
    lane = lax.broadcasted_iota(jnp.int32, (1, WSLOT), 1)
    sub = lax.broadcasted_iota(jnp.int32, (WSLOT, D), 0)
    half = WSLOT // 2
    if shifted:
        first, second = lens(win) - half, lens(win + 1) + half
        ml = lane < jnp.where(lane < half, first, second)
        ms = sub < jnp.where(sub < half, first, second)
    else:
        ml = lane < lens(win)
        ms = sub < lens(win)
    return ml.astype(f32), ms


def head_diag(a, b):
    zero = jnp.zeros((HD, WSLOT), a.dtype)
    return jnp.concatenate([cat([a, zero]), cat([zero, b])], axis=0)


def two_blocks(a, b):
    zero = jnp.zeros(a.shape, a.dtype)
    return jnp.concatenate([cat([a, zero]), cat([zero, b])], axis=0)


def quad_diag(o, ml):
    return jnp.concatenate([o[0 : 2 * HD, 0:WSLOT] * ml, o[2 * HD :, WSLOT:] * ml], axis=0)


def even_odd(heads):
    zero = jnp.zeros((HD, WSLOT), heads[0].dtype)
    return jnp.concatenate(
        [cat([zero, t] if h % 2 else [t, zero]) for h, t in enumerate(heads)], axis=0
    )


def pair_lhs(t, cols):
    return jnp.concatenate([t * cols[p] for p in range(NPAIR)], axis=0)


def head_rows(t):
    return [t[h * HD : (h + 1) * HD] for h in range(HEADS)]


def pair_rows(t, p):
    return t[2 * p * HD : (2 * p + 1) * HD], t[(2 * p + 1) * HD : (2 * p + 2) * HD]


class Values:
    def __init__(self):
        self.d = {}

    def put(self, name, i, value):
        self.d[name, i] = value

    def get(self, name, i):
        return self.d[name, i]


STASH = {
    "xb": (20, (D, 2 * WSLOT), bf16),
    "nb": (20, (D, 2 * WSLOT), bf16),
    "q": (40, (D, WSLOT), bf16),
    "k": (40, (D, WSLOT), bf16),
    "v": (40, (D, WSLOT), bf16),
    "mix": (40, (D, WSLOT), f32),
    "xh1": (40, (D, WSLOT), f32),
    "xh2": (40, (D, WSLOT), f32),
    "dg": (40, (FF, WSLOT), bf16),
    "ia": (40, (FF, WSLOT), bf16),
    "e": (80, (2 * WSLOT, 2 * WSLOT), bf16),
    "rden": (20, (8, 2 * WSLOT), f32),
    "rs1": (20, (8, WSLOT), f32),
    "rs2": (20, (8, WSLOT), f32),
}
ROWS_OF_ONE = ("rden", "rs1", "rs2")


def stash_scratch(nw):
    return [pltpu.VMEM((n * nw // 40, *s), t) for n, s, t in STASH.values()]


class Stash:
    def __init__(self, refs, pair):
        self.refs = dict(zip(STASH, refs))
        self.pair = pair

    def at(self, name, i):
        count = STASH[name][0] // 20
        ref = self.refs[name]
        if name in ROWS_OF_ONE:
            return ref, (self.pair, slice(i, i + 1), slice(None))
        return ref, (self.pair * count + i,)

    def put(self, name, i, value):
        ref, at = self.at(name, i)
        ref[at] = value

    def get(self, name, i):
        ref, at = self.at(name, i)
        return ref[at]


def interleave(gens):
    free = {"m": 0, "v": 0}
    ready = [0] * len(gens)
    ahead = {}
    for c, gen in enumerate(gens):
        ahead[c] = next(gen)
    while ahead:
        c = min(ahead, key=lambda i: (max(free[ahead[i][0]], ready[i]), i))
        kind, cost = ahead[c]
        start = max(free[kind], ready[c])
        free[kind] = start + cost
        ready[c] = start + cost + (LATENCY if kind == "m" else LATENCY // 4)
        try:
            ahead[c] = next(gens[c])
        except StopIteration:
            del ahead[c]


def forward(xs, masks, row0, s, keep):
    wqt, wot, wit, wbt, vec, cols = s
    two = range(2)
    yield "m", 96
    xb = cat(xs).astype(bf16)
    keep.put("xb", 0, xb)
    packed = dot(wqt[...], xb)
    kns, ones, qs, vs = [], [], [], []
    for i in two:
        yield "v", 45
        ml, ms = masks[i]
        pk = packed[:, i * WSLOT : (i + 1) * WSLOT]
        q = (pk[0:D] + vec[PQ]).astype(bf16)
        kf = pk[D : 2 * D] * (ml * LOG2E)
        v = ((pk[2 * D :] + vec[PV]) * ml).astype(bf16)
        k = kf.astype(bf16)
        kn = k.T.astype(f32)
        kn = jnp.where(ms, kn, jnp.broadcast_to(kn[row0 : row0 + 1, :], kn.shape))
        kns.append(kn.astype(bf16))
        mrow = jnp.broadcast_to(ml, (8, WSLOT))
        mzero = jnp.zeros((8, WSLOT), f32)
        ones.append(
            jnp.concatenate([cat([mrow, mzero]), cat([mzero, mrow])], axis=0).astype(bf16)
        )
        qs.append(q)
        vs.append(v)
        keep.put("q", i, q)
        keep.put("k", i, k)
        keep.put("v", i, v)
    items = [(i, u) for i in two for u in range(NQUAD)]
    scores, exps, mixes = {}, {}, {}

    def weigh(t):
        i, u = items[t]
        v4 = vs[i][u * 4 * HD : (u + 1) * 4 * HD]
        lhs = jnp.concatenate([two_blocks(v4[0 : 2 * HD], v4[2 * HD :]), ones[i]], axis=0)
        o = dot(lhs, exps.pop(t))
        parts = []
        for p in range(2):
            den = o[4 * HD + 8 * p : 4 * HD + 8 * p + 1, :]
            rden = 1.0 / den
            keep.put("rden", 2 * t + p, rden)
            rows = o[2 * p * HD : (2 * p + 2) * HD]
            parts += [rows[0:HD, 0:WSLOT] * rden[:, 0:WSLOT], rows[HD:, WSLOT:] * rden[:, WSLOT:]]
        mixes[t] = jnp.concatenate(parts, axis=0)

    for t, (i, u) in enumerate(items):
        if u == 0:
            yield "m", 128
            scores[i] = dot(pair_lhs(kns[i], cols), even_odd(head_rows(qs[i])))
        es = []
        for p in (2 * u, 2 * u + 1):
            yield "v", 35
            sc = scores[i][p * WSLOT : (p + 1) * WSLOT]
            es.append(jnp.exp2((sc - jnp.max(sc, axis=0, keepdims=True)).astype(bf16)))
        exps[t] = jnp.concatenate(es, axis=0)
        keep.put("e", t, exps[t])
        yield "m", 64
        weigh(t)
    mix = [jnp.concatenate([mixes[i * NQUAD + u] for u in range(NQUAD)], axis=0) for i in two]
    for i in two:
        keep.put("mix", i, mix[i])
    yield "m", 32
    branch = dot(wot[...], cat(mix).astype(bf16))
    normed = []
    for i in two:
        yield "v", 50
        first = xs[i] + (branch[:, i * WSLOT : (i + 1) * WSLOT] + vec[PO])
        xh, rs = norm0(first)
        keep.put("xh1", i, xh)
        keep.put("rs1", i, rs)
        normed.append(xh * vec[PGA] + vec[PBA])
    yield "m", 64
    nb = cat(normed).astype(bf16)
    keep.put("nb", 0, nb)
    pre = dot(wit[...], nb)
    inner = []
    for i in two:
        acts, grads = [], []
        for r in range(0, FF, GROW):
            if r % (2 * GROW) == 0:
                yield "v", 50
            bias = vec[PI0 + r // D, r % D : r % D + GROW, :]
            act, grad = gelu_low(pre[r : r + GROW, i * WSLOT : (i + 1) * WSLOT] + bias)
            acts.append(act)
            grads.append(grad)
        inner.append(jnp.concatenate(acts, axis=0))
        keep.put("ia", i, inner[i])
        keep.put("dg", i, jnp.concatenate(grads, axis=0))
    yield "m", 64
    outer = dot(wbt[...], cat(inner))
    out = []
    for i in two:
        yield "v", 55
        second = normed[i] + (outer[:, i * WSLOT : (i + 1) * WSLOT] + vec[PB])
        xh, rs = norm0(second)
        keep.put("xh2", i, xh)
        keep.put("rs2", i, rs)
        out.append((xh * vec[PGF] + vec[PBF]) * masks[i][0])
    return out


def backward(des, masks, layer, w, s, acc, keep):
    w_qkv, w_out, w_in, w_back = w[0], w[2], w[6], w[8]
    a_qkv, a_out, a_in, a_back, a_vec = acc
    vec, cols = s[4:6]
    two = range(2)
    ones = jnp.ones((16, 2 * WSLOT), bf16)
    d_second = []
    for i in two:
        yield "v", 65
        dy = des[i] * masks[i][0]
        xh = keep.get("xh2", i)
        a_vec[0] += dy * xh
        a_vec[1] += dy
        d_second.append(norm0_back(dy * vec[PGF], xh, keep.get("rs2", i)))
    yield "m", 64
    do = cat(d_second).astype(bf16)
    d_act = dot(w_back[layer], do)
    yield "m", 64
    inner = cat([keep.get("ia", i) for i in two])
    a_back[...] += dot_nt(jnp.concatenate([inner, ones], axis=0), do)
    dis = []
    for i in two:
        yield "v", 25
        d = d_act[:, i * WSLOT : (i + 1) * WSLOT].astype(bf16)
        dis.append(keep.get("dg", i) * d)
    yield "m", 64
    di = cat(dis)
    dn = dot(w_in[layer], di)
    yield "m", 64
    a_in[...] += dot_nt(jnp.concatenate([keep.get("nb", 0), ones], axis=0), di)
    d_first = []
    for i in two:
        yield "v", 70
        d = d_second[i] + dn[:, i * WSLOT : (i + 1) * WSLOT]
        xh = keep.get("xh1", i)
        a_vec[2] += d * xh
        a_vec[3] += d
        d_first.append(norm0_back(d * vec[PGA], xh, keep.get("rs1", i)))
    yield "m", 32
    db = cat(d_first).astype(bf16)
    dm = dot(w_out[layer], db)
    yield "m", 64
    mixb = cat([keep.get("mix", i) for i in two]).astype(bf16)
    a_out[...] += dot_nt(jnp.concatenate([mixb, ones], axis=0), db)
    items = [(i, u) for i in two for u in range(NQUAD)]
    dps, dms, rowdots, dqs, dks, dvs = {}, {}, {}, {}, {}, {}
    for t, (i, u) in enumerate(items):
        if u == 0:
            yield "v", 25
            heads, dots = [], []
            grad = head_rows(dm[:, i * WSLOT : (i + 1) * WSLOT])
            mix = head_rows(keep.get("mix", i))
            for h in range(HEADS):
                rden = keep.get("rden", i * NPAIR + h // 2)
                d = grad[h] * rden[:, (h % 2) * WSLOT : (h % 2 + 1) * WSLOT]
                dots.append(jnp.sum(d * mix[h], axis=0, keepdims=True))
                heads.append(d.astype(bf16))
            dms[i], rowdots[i] = heads, dots
            yield "m", 128
            dps[i] = dot(pair_lhs(keep.get("v", i).T, cols), even_odd(heads))
        yield "m", 64
        e = keep.get("e", t)
        heads = dms[i][4 * u : 4 * u + 4]
        dd = jnp.concatenate([head_diag(*heads[0:2]), head_diag(*heads[2:4])], axis=0)
        dvs[t] = quad_diag(dot_nt(dd, e), masks[i][0])
        ds = []
        for p in range(2):
            yield "v", 25
            h = 4 * u + 2 * p
            dp = dps[i][(2 * u + p) * WSLOT : (2 * u + p + 1) * WSLOT]
            rowdot = cat(rowdots[i][h : h + 2])
            ds.append(e[p * WSLOT : (p + 1) * WSLOT] * (dp - rowdot).astype(bf16))
        ds = jnp.concatenate(ds, axis=0)
        yield "m", 64
        k4 = keep.get("k", i)[u * 4 * HD : (u + 1) * 4 * HD]
        o = dot(two_blocks(k4[0 : 2 * HD], k4[2 * HD :]), ds)
        o = [o[j * HD : (j + 1) * HD, (j % 2) * WSLOT : (j % 2 + 1) * WSLOT] for j in range(4)]
        dqs[t] = jnp.concatenate(o, axis=0) * (HD ** (-0.5) / LOG2E)
        yield "m", 64
        heads = head_rows(keep.get("q", i))[4 * u : 4 * u + 4]
        q = jnp.concatenate([head_diag(*heads[0:2]), head_diag(*heads[2:4])], axis=0)
        dks[t] = quad_diag(dot_nt(q, ds), masks[i][0])

    def whole(d):
        return cat(
            [jnp.concatenate([d[i * NQUAD + u] for u in range(NQUAD)], axis=0) for i in two]
        ).astype(bf16)

    yield "m", 96
    dpk = jnp.concatenate([whole(dqs), whole(dks), whole(dvs)], axis=0)
    dx = dot(w_qkv[layer], dpk)
    yield "m", 128
    a_qkv[...] += dot_nt(jnp.concatenate([keep.get("xb", 0), ones], axis=0), dpk)
    yield "v", 20
    return [d_first[i] + dx[:, i * WSLOT : (i + 1) * WSLOT] for i in two]


ACC_SHAPES = [(D + 16, 3 * D), (D + 16, D), (D + 16, FF), (FF + 16, D), (4, D, D)]


def clear(acc):
    for a in acc:
        a[...] = jnp.zeros(a.shape, f32)


def shift_tile(left, right):
    half = WSLOT // 2
    lane = lax.broadcasted_iota(jnp.int32, left.shape, 1)
    return pltpu.roll(jnp.where(lane < half, right, left), half, 1)


def encoded_pair(ps, coef, w0):
    out = []
    for i in range(2):
        at = pl.ds(pl.multiple_of((w0 + i) * WSLOT, WSLOT), WSLOT)
        out.append((ps[at, :] * coef).T)
    return out


def first_forward_step(g, w0, lens, ps, coef, tiles, s, stash):
    def chain(c):
        w = w0 + 2 * c
        masks = [window_masks(False, lens, w + i) for i in range(2)]
        keep = Values() if stash is None else Stash(stash, w // 2)
        out = yield from forward(encoded_pair(ps, coef, w), masks, 0, s, keep)
        for i in range(2):
            tiles[w + i] = out[i]

    interleave([chain(c) for c in range(g // 2)])


def second_step(g, w0, lens, tiles, cots, out_rows, gv, gv0, w, s, acc):
    def chain(c):
        v = w0 + 2 * c
        masks = [window_masks(True, lens, v + i) for i in range(2)]
        ts = [tiles[v + i] for i in range(3)]
        xs = [shift_tile(ts[i], ts[i + 1]) for i in range(2)]
        keep = Values()
        out = yield from forward(xs, masks, WSLOT // 2, s, keep)
        for i in range(2):
            out_rows(v + i, out[i].astype(bf16).T)
        des = [cots(v + i).T.astype(f32) for i in range(2)]
        dx = yield from backward(des, masks, 1, w, s, acc, keep)
        for i in range(2):
            gv[gv0 + v + i] = dx[i]

    interleave([chain(c) for c in range(g // 2)])


def first_backward_step(g, w0, lens, ps, coef, gv, put_grad, w, s, acc, stash):
    def chain(c):
        v = w0 + 2 * c
        masks = [window_masks(False, lens, v + i) for i in range(2)]
        if stash is None:
            keep = Values()
            yield from forward(encoded_pair(ps, coef, v), masks, 0, s, keep)
        else:
            keep = Stash(stash, v // 2)
        ts = [gv[v + i] for i in range(3)]
        des = [shift_tile(ts[i], ts[i + 1]) for i in range(2)]
        dx = yield from backward(des, masks, 0, w, s, acc, keep)
        for i in range(2):
            put_grad(v + i, dx[i].T)

    interleave([chain(c) for c in range(g // 2)])


def row_block(ref, start):
    return ref[pl.ds(pl.multiple_of(start, WSLOT // 2), WSLOT), :]


def first_forward_kernel(nw, g, lens, ps, coef, *refs):
    w, out, s = refs[:12], refs[12], refs[13:]
    prepare(0, w, s)

    def body(j, _):
        first_forward_step(g, g * j, lambda i: lens[i], ps, coef[...], out, s, None)
        return 0

    lax.fori_loop(0, nw // g, body, 0)


def second_kernel(nw, g, lens, fo, rim, cot, rim_cot, *refs):
    w = refs[:12]
    out, gv = refs[12:14]
    acc = refs[14:19]
    s = refs[19:25]
    tiles, cots = refs[25:27]
    prepare(1, w, s)
    clear(acc)
    half = WSLOT // 2
    tiles[0:nw] = fo[...]
    tiles[nw] = rim[...].astype(f32)
    n = nw * WSLOT
    cots[0 : n - half, :] = cot[half:, :]
    cots[n - half :, :] = rim_cot[...]

    def put(win, rows):
        out[pl.ds(pl.multiple_of(win * WSLOT, WSLOT), WSLOT), :] = rows

    def body(j, _):
        second_step(
            g, g * j, lambda i: lens[i], tiles, lambda i: row_block(cots, i * WSLOT), put, gv, 0,
            w, s, acc,
        )
        return 0

    lax.fori_loop(0, nw // g, body, 0)


def first_backward_kernel(nw, g, lens, ps, coef, gv, back, *refs):
    w = refs[:12]
    d_enc = refs[12]
    acc = refs[13:18]
    s = refs[18:24]
    tiles = refs[24]
    prepare(0, w, s)
    clear(acc)
    tiles[1 : nw + 1] = gv[...]
    tiles[0] = back[...].astype(f32)

    def put_grad(win, rows):
        d_enc[pl.ds(pl.multiple_of(win * WSLOT, WSLOT), WSLOT), :] = rows

    def body(j, _):
        first_backward_step(
            g, g * j, lambda i: lens[i], ps, coef[...], tiles, put_grad, w, s, acc, None
        )
        return 0

    lax.fori_loop(0, nw // g, body, 0)


def chunks(bucket):
    step = 2 * D if bucket % (2 * D) == 0 else bucket
    return [slice(c, c + step) for c in range(0, bucket, step)]


def scatter_kernel(nw, slots, lens, feats, w, b, ps, stat, hid, *accs):
    tiles, _, bucket = feats.shape
    pitch = slots.shape[0] // tiles
    rows = accs[0].shape[0]

    def zero(i, _):
        for a in accs:
            a[pl.ds(pl.multiple_of(i * 128, 128), 128), :] = jnp.zeros((128, D), f32)
        return 0

    lax.fori_loop(0, rows // 128, zero, 0)

    def one_bucket(t, _):
        parts = chunks(bucket)
        pres = [dot_tn(feats[t, :, at], w[...]) for at in parts]
        for at, pre in zip(parts, pres):
            hid[at, :] = gelu(pre + b[...])

        def some(i, _):
            base = i * 8
            for u in range(0, 8, NACC // 2):
                at, h = [], []
                for a in range(NACC // 2):
                    for far, r in enumerate(both_slots(slots[t * pitch + base + u + a])):
                        at.append(pl.ds(r, 1))
                        h.append(hid[pl.ds(far * (bucket // 2) + base + u + a, 1), :])
                new = [accs[a][at[a], :] + h[a] for a in range(NACC)]
                for a in range(NACC):
                    accs[a][at[a], :] = new[a]
            return 0

        lax.fori_loop(0, bucket // 16, some, 0)
        return 0

    lax.fori_loop(0, tiles, one_bucket, 0)

    sub = lax.broadcasted_iota(jnp.int32, (WSLOT, D), 0)

    def finish(j, carry):
        sq, cnt = carry
        for win in range(2):
            win = 2 * j + win
            at = pl.ds(pl.multiple_of(win * WSLOT, WSLOT), WSLOT)
            total = accs[0][at, :]
            for a in accs[1:]:
                total = total + a[at, :]
            ps[at, :] = total
            valid = (sub < lens[0, win]).astype(f32)
            sq, cnt = sq + valid * total * total, cnt + valid
        return sq, cnt

    z = jnp.zeros((WSLOT, D), f32)
    sq, cnt = lax.fori_loop(0, nw // 2, finish, (z, z))
    stat[...] = jnp.zeros(stat.shape, f32)
    stat[0:1, :] = jnp.sum(sq, axis=0, keepdims=True)
    stat[1:2, :] = jnp.sum(cnt, axis=0, keepdims=True)


def point_bucket(t, slots, feats, w, b, dp, got, put, gw, gb):
    tiles, _, bucket = feats.shape
    pitch = slots.shape[0] // tiles

    def some(i, _):
        for base in range(0, 32, 16):
            at = i * 32 + base
            words = [both_slots(slots[t * pitch + at + u]) for u in range(16)]
            new = [dp[pl.ds(r, 1), :] for word in words for r in word]
            for u in range(16):
                for far in range(2):
                    got[pl.ds(far * (bucket // 2) + at + u, 1), :] = new[2 * u + far]
        return 0

    lax.fori_loop(0, bucket // 64, some, 0)
    for u in range(bucket // 64 * 32, bucket // 2):
        for far, row in enumerate(both_slots(slots[t * pitch + u])):
            at = far * (bucket // 2) + u
            got[at : at + 1, :] = dp[pl.ds(row, 1), :]

    parts = chunks(bucket)
    fts = [feats[t, :, at] for at in parts]
    pres = [dot_tn(ft, w[...]) for ft in fts]
    dpres = [
        gelu_low(pre + b[...])[1] * got[at, :].astype(bf16) for at, pre in zip(parts, pres)
    ]
    for at, dpre in zip(parts, dpres):
        put(t, at, dot_nt(w[...], dpre).astype(bf16))
    total = dot(fts[0], dpres[0])
    for ft, dpre in zip(fts[1:], dpres[1:]):
        total = total + dot(ft, dpre)
    gw[...] += total
    for dpre in dpres:
        gb[...] += jnp.sum(dpre.astype(f32).reshape(dpre.shape[0] // 8, 8, D), axis=0)


def gather_kernel(nw, slots, lens, feats, w, b, d_enc, ps, ca, cb, out, gw, gb, dp, got):
    tiles, _, bucket = feats.shape
    sub = lax.broadcasted_iota(jnp.int32, (WSLOT, D), 0)

    def make(win, _):
        at = pl.ds(pl.multiple_of(win * WSLOT, WSLOT), WSLOT)
        valid = (sub < lens[0, win]).astype(f32)
        dp[at, :] = d_enc[at, :] * ca[...] - ps[at, :] * valid * cb[...]
        return 0

    lax.fori_loop(0, nw, make, 0)
    dp[nw * WSLOT : nw * WSLOT + 128, :] = jnp.zeros((128, D), f32)
    gw[...] = jnp.zeros(gw.shape, f32)
    gb[...] = jnp.zeros(gb.shape, f32)

    def put(t, at, rows):
        out[t, :, at] = rows

    def one_bucket(t, _):
        point_bucket(t, slots, feats, w, b, dp, got, put, gw, gb)
        return 0

    lax.fori_loop(0, tiles, one_bucket, 0)


EXTRA = 64
VFE_ROW = 32
MESH = pl.DeviceIdType.MESH


def peers(axis, count):
    me = lax.axis_index(axis)
    return me, [lax.rem(me + d, count) for d in range(1, count)]


def remote(src, dst, send, recv, axis, peer):
    return pltpu.make_async_remote_copy(
        src_ref=src, dst_ref=dst, send_sem=send, recv_sem=recv,
        device_id={axis: peer}, device_id_type=MESH,
    )


def far_first(d, count):
    near = lax.div(d + 1, 2)
    return lax.rem(count // 2 + jnp.where(lax.rem(d, 2) == 0, near, count - near), count)


def start_all(copies):
    for c in copies:
        c.start()


def wait_all(copies):
    for c in copies:
        c.wait()


def greet(axes):
    barrier = pltpu.get_barrier_semaphore()
    for axis, count in axes:
        for peer in peers(axis, count)[1]:
            pl.semaphore_signal(barrier, 1, device_id={axis: peer}, device_id_type=MESH)
    pl.semaphore_wait(barrier, sum(count - 1 for _, count in axes))


def blocks(acc):
    a_qkv, a_out, a_in, a_back, _ = acc
    return (
        [a_qkv[0:D, i * D : (i + 1) * D] for i in range(3)]
        + [a_out[0:D, :]]
        + [a_in[0:D, i * D : (i + 1) * D] for i in range(2)]
        + [a_back[i * D : (i + 1) * D, :] for i in range(2)]
    )


class Reducer:
    ROWS = 8 * D

    def __init__(self, frames, tiles, refs, full):
        self.frames, self.tiles, self.full = frames, tiles, full
        self.mine, self.got1, self.part, self.got2, self.ss, self.rs = refs
        self.me_f, self.peers_f = peers("frame", frames)
        self.me_t, self.peers_t = peers("tile", tiles)
        per = self.part.shape[1]
        self.here = pl.ds(pl.multiple_of(self.me_t * per, per), per)

    @staticmethod
    def scratch(frames, tiles):
        per_f = Reducer.ROWS // frames
        per_t = per_f // tiles
        count = 2 * (frames - 1) + 2 * (tiles - 1)
        return [
            pltpu.VMEM((frames, per_f, D), bf16),
            pltpu.VMEM((frames - 1, per_f, D), bf16),
            pltpu.VMEM((tiles, per_t, D), bf16),
            pltpu.VMEM((tiles - 1, per_t, D), bf16),
            pltpu.SemaphoreType.DMA((count,)),
            pltpu.SemaphoreType.DMA((count,)),
        ]

    def copies(self, stage):
        axis = "frame" if stage in (0, 3) else "tile"
        prs = self.peers_f if axis == "frame" else self.peers_t
        f, t = self.frames - 1, self.tiles - 1
        at = (0, f, f + t, f + 2 * t)[stage]
        out = []
        for i, p in enumerate(prs):
            if stage == 0:
                src, dst = self.mine.at[p], self.got1.at[i]
            elif stage == 1:
                src, dst = self.part.at[p], self.got2.at[i]
            elif stage == 2:
                src = dst = self.full.at[self.me_f, self.here, :]
            else:
                src = dst = self.full.at[self.me_f]
            out.append(remote(src, dst, self.ss.at[at + i], self.rs.at[at + i], axis, p))
        return out

    def step1(self, acc):
        per = self.mine.shape[1]
        for i, block in enumerate(blocks(acc)):
            r = i * D
            self.mine[r // per, r % per : r % per + D, :] = block.astype(bf16)
        start_all(self.copies(0))

    def step2(self):
        wait_all(self.copies(0))
        total = self.mine[self.me_f].astype(f32)
        for i in range(self.frames - 1):
            total = total + self.got1[i].astype(f32)
        self.part[...] = total.astype(bf16).reshape(self.part.shape)
        start_all(self.copies(1))

    def step3(self):
        wait_all(self.copies(1))
        total = self.part[self.me_t].astype(f32)
        for i in range(self.tiles - 1):
            total = total + self.got2[i].astype(f32)
        self.full[self.me_f, self.here, :] = total.astype(bf16)
        start_all(self.copies(2))

    def step4(self):
        wait_all(self.copies(2))
        start_all(self.copies(3))

    def step5(self):
        wait_all(self.copies(3))


def extra_rows(acc):
    a_qkv, a_out, a_in, a_back, a_vec = acc
    r = [a_qkv[D : D + 1, i * D : (i + 1) * D] for i in range(3)]
    r.append(a_out[D : D + 1, :])
    r += [jnp.sum(a_vec[i].T, axis=0, keepdims=True) for i in (2, 3)]
    r += [a_in[D : D + 1, i * D : (i + 1) * D] for i in range(2)]
    r.append(a_back[FF : FF + 1, :])
    r += [jnp.sum(a_vec[i].T, axis=0, keepdims=True) for i in (0, 1)]
    r.append(jnp.zeros((5, D), f32))
    return jnp.concatenate(r, axis=0)


def slot_rows(bucket):
    return -(-bucket // (16 * D)) * 8


def both_slots(word):
    return word & 0xFFFF, lax.shift_right_logical(word, 16)


def exchange_kernel(tiles, n, blen, wlen, slot, feats, got_feats, got_slots, next_len, *scr):
    fbuf, tslot, lbuf, ss, rs, ss2, rs2, ss3, rs3 = scr
    bucket = fbuf.shape[2]
    me, prs = peers("tile", tiles)
    for t in range(tiles):
        fbuf[t] = feats[0, :, t * bucket : (t + 1) * bucket]
    greet((("tile", tiles),))
    points = [
        remote(fbuf.at[p], got_feats.at[me], ss.at[i], rs.at[i], "tile", p)
        for i, p in enumerate(prs)
    ]
    order = sorted(range(tiles - 1), key=lambda i: abs(2 * (i + 1) - tiles))
    start_all([points[i] for i in order])
    lane = lax.broadcasted_iota(jnp.int32, (1, D), 1)
    rows = tslot.shape[1]
    for t in range(tiles):
        parts = [
            jnp.where(lane + c < blen[0, t], slot[:, t * bucket + c : t * bucket + c + D], n)
            for c in range(0, bucket, D)
        ]
        half = len(parts) // 2
        parts = [a + b * 65536 for a, b in zip(parts[:half], parts[half:])]
        parts.append(jnp.full((rows - half, D), n, jnp.int32))
        tslot[t] = jnp.concatenate(parts, axis=0)
    slots = [
        remote(tslot.at[p], got_slots.at[me], ss2.at[i], rs2.at[i], "tile", p)
        for i, p in enumerate(prs)
    ]
    start_all([slots[i] for i in order])
    lbuf[...] = jnp.full(lbuf.shape, wlen[0, 0], jnp.int32)
    lens = remote(lbuf, next_len, ss3.at[0], rs3.at[0], "tile", lax.rem(me + tiles - 1, tiles))
    lens.start()
    got_feats[me] = fbuf[me]
    got_slots[me] = tslot[me]
    wait_all(points + slots + [lens])


def main_scratch(frames, tiles, nw, pf, bucket):
    n = nw * WSLOT
    half = WSLOT // 2
    dma = pltpu.SemaphoreType.DMA
    return {
        "s0": layer_scratch(),
        "s1": layer_scratch(),
        "a0": [pltpu.VMEM(a, f32) for a in ACC_SHAPES],
        "a1": [pltpu.VMEM(a, f32) for a in ACC_SHAPES],
        "stash": stash_scratch(nw),
        "tiles": [pltpu.VMEM((nw + 1, D, WSLOT), f32)],
        "gv": [pltpu.VMEM((nw + 1, D, WSLOT), f32)],
        "rim": [pltpu.VMEM((D, WSLOT), bf16)] * 4,
        "po": [pltpu.VMEM((n + half, D), bf16)],
        "cot": [pltpu.VMEM((n + half, D), bf16)],
        "dp": [pltpu.VMEM((n + WSLOT, D), f32)],
        "dot": [pltpu.VMEM((WSLOT, D), f32)],
        "got": [pltpu.VMEM((bucket, D), f32)],
        "gout": [pltpu.VMEM((tiles, pf, bucket), bf16)],
        "gw": [pltpu.VMEM((pf, D), f32), pltpu.VMEM((8, D), f32)],
        "xstat": [pltpu.VMEM((tiles, 8, D), f32), dma((tiles - 1,)), dma((tiles - 1,))],
        "xdot": [pltpu.VMEM((tiles, 8, D), f32), dma((tiles - 1,)), dma((tiles - 1,))],
        "rsem": [dma((4,)), dma((4,))],
        "gsem": [dma((tiles - 1,)), dma((tiles - 1,))],
        "own": [dma((3,))],
        "r0": Reducer.scratch(frames, tiles),
        "r1": Reducer.scratch(frames, tiles),
        "x0": FrameTile.scratch(frames, tiles, VFE_ROW),
        "x1": FrameTile.scratch(frames, tiles, 24),
    }


def split_refs(spec, refs):
    out, at = {}, 0
    for name, entries in spec.items():
        out[name] = refs[at : at + len(entries)]
        at += len(entries)
    return out


class FrameTile:
    def __init__(self, frames, tiles, refs):
        self.x1, self.x2, self.ss, self.rs = refs
        self.frames, self.tiles = frames, tiles
        self.me_f, self.prs_f = peers("frame", frames)
        self.me_t, self.prs_t = peers("tile", tiles)

    @staticmethod
    def scratch(frames, tiles, rows):
        count = frames + tiles - 2
        return [
            pltpu.VMEM((frames, rows, D), f32), pltpu.VMEM((tiles, rows, D), f32),
            pltpu.SemaphoreType.DMA((count,)), pltpu.SemaphoreType.DMA((count,)),
        ]

    def copies(self, axis):
        if axis == "frame":
            at, view, prs = 0, self.x1.at[self.me_f], self.prs_f
        else:
            at, view, prs = self.frames - 1, self.x2.at[self.me_t], self.prs_t
        return [
            remote(view, view, self.ss.at[at + i], self.rs.at[at + i], axis, p)
            for i, p in enumerate(prs)
        ]

    def start(self, value):
        self.x1[self.me_f] = value
        start_all(self.copies("frame"))

    def middle(self):
        wait_all(self.copies("frame"))
        total = self.x1[0]
        for f in range(1, self.frames):
            total = total + self.x1[f]
        self.x2[self.me_t] = total
        start_all(self.copies("tile"))

    def total(self):
        wait_all(self.copies("tile"))
        total = self.x2[0]
        for t in range(1, self.tiles):
            total = total + self.x2[t]
        return total


class All:
    def __init__(self, tiles, refs):
        self.buf, self.ss, self.rs = refs
        self.tiles = tiles
        self.me, self.prs = peers("tile", tiles)

    def copies(self):
        view = self.buf.at[self.me]
        return [
            remote(view, view, self.ss.at[i], self.rs.at[i], "tile", p)
            for i, p in enumerate(self.prs)
        ]

    def start(self, value):
        self.buf[self.me] = value
        start_all(self.copies())

    def total(self):
        wait_all(self.copies())
        total = self.buf[0]
        for t in range(1, self.tiles):
            total = total + self.buf[t]
        return total


def main_kernel(frames, tiles, nw, g, spec, *refs):
    slots, wlen, next_len, cot, stat, ps, feats, w_vfe, b_vfe, gain = refs[:10]
    w = refs[10:22]
    pillar_out, gp, full0, full1, small = refs[22:27]
    r = split_refs(spec, refs[27:])
    n = nw * WSLOT
    half = WSLOT // 2
    bucket = feats.shape[2]
    pitch = slots.shape[0] // tiles
    groups = nw // g
    me_t, prs_t = peers("tile", tiles)
    me_f, prs_f = peers("frame", frames)
    before, after = lax.rem(me_t + tiles - 1, tiles), lax.rem(me_t + 1, tiles)
    greet((("frame", frames), ("tile", tiles)))

    (cotx,), (own,) = r["cot"], r["own"]
    stats = All(tiles, r["xstat"])
    stats.start(stat[...])
    rss, rrs = r["rsem"]
    cot_rim = remote(
        cot.at[0, 0:half, :], cotx.at[n : n + half, :], rss.at[0], rrs.at[0], "tile", before
    )
    cot_rim.start()
    cot_own = pltpu.make_async_copy(cot.at[0], cotx.at[0:n, :], own.at[0])
    cot_own.start()
    s0, s1, a0, a1 = r["s0"], r["s1"], r["a0"], r["a1"]
    prepare(0, w, s0)
    prepare(1, w, s1)
    clear(a0)
    clear(a1)
    sums = stats.total()
    count = sums[1:2, :]
    scale = lax.rsqrt(sums[0:1, :] / count + EPS)
    coef = scale * gain[...]

    def lens(i):
        return jnp.where(i < nw, wlen[0, jnp.minimum(i, nw - 1)], next_len[0, 0])

    (fo,), (gv,), (po,) = r["tiles"], r["gv"], r["po"]
    rim_out, rim_in, gv_out, gv_in = r["rim"]

    def rim_copy():
        return remote(rim_out, rim_in, rss.at[1], rrs.at[1], "tile", before)

    def fwd(j, _):
        first_forward_step(g, g * j, lens, ps, coef, fo, s0, r["stash"])

        @pl.when(j == 0)
        def _():
            rim_out[...] = fo[0].astype(bf16)
            rim_copy().start()

        return 0

    lax.fori_loop(0, groups, fwd, 0)
    rim_copy().wait()
    fo[nw] = rim_in[...].astype(f32)
    cot_rim.wait()
    cot_own.wait()

    def gv_copy():
        return remote(gv_out, gv_in, rss.at[2], rrs.at[2], "tile", after)

    def po_copy():
        return remote(
            po.at[n : n + half, :], pillar_out.at[0:half, :], rss.at[3], rrs.at[3], "tile", after
        )

    def put_rows(win, rows):
        po[pl.ds(pl.multiple_of(win * WSLOT + half, half), WSLOT), :] = rows

    def second(j, _):
        w0 = g * lax.rem(j + groups - 1, groups)
        second_step(
            g, w0, lens, fo, lambda i: row_block(cotx, i * WSLOT + half), put_rows, gv, 1,
            w, s1, a1,
        )

        @pl.when(j == 0)
        def _():
            gv_out[...] = gv[nw].astype(bf16)
            gv_copy().start()
            po_copy().start()

        return 0

    lax.fori_loop(0, groups, second, 0)
    po_own = pltpu.make_async_copy(po.at[half:n, :], pillar_out.at[half:n, :], own.at[1])
    po_own.start()
    lay1 = Reducer(frames, tiles, r["r1"], full1)
    lay1.step1(a1)
    gv_copy().wait()
    gv[0] = gv_in[...].astype(f32)
    (dp,), (dot_acc,) = r["dp"], r["dot"]
    dot_acc[...] = jnp.zeros(dot_acc.shape, f32)

    def put_grad(win, rows):
        at = pl.ds(pl.multiple_of(win * WSLOT, WSLOT), WSLOT)
        dp[at, :] = rows
        dot_acc[...] += rows * ps[at, :]

    def bwd(j, _):
        first_backward_step(g, g * j, lens, ps, coef, gv, put_grad, w, s0, a0, r["stash"])
        for at, step in ((1, lay1.step2), (2, lay1.step3), (3, lay1.step4)):
            pl.when(j == at)(step)
        return 0

    lax.fori_loop(0, groups, bwd, 0)

    local_dot = jnp.sum(dot_acc[...], axis=0, keepdims=True)
    dots = All(tiles, r["xdot"])
    dots.start(jnp.broadcast_to(local_dot, (8, D)))
    lay0 = Reducer(frames, tiles, r["r0"], full0)
    lay0.step1(a0)
    early, late = FrameTile(frames, tiles, r["x0"]), FrameTile(frames, tiles, r["x1"])
    early.start(jnp.concatenate([extra_rows(a0), extra_rows(a1)], axis=0))
    (got,), (gout,), (gw, gb) = r["got"], r["gout"], r["gw"]
    gw[...] = jnp.zeros(gw.shape, f32)
    gb[...] = jnp.zeros(gb.shape, f32)
    dp[n:, :] = jnp.zeros((WSLOT, D), f32)
    cb = gain[...] * scale * scale * scale * dots.total()[0:1, :] / count
    sub = lax.broadcasted_iota(jnp.int32, (WSLOT, D), 0)

    def make(j, _):
        for win in range(4):
            win = 4 * j + win
            at = pl.ds(pl.multiple_of(win * WSLOT, WSLOT), WSLOT)
            valid = (sub < wlen[0, win]).astype(f32)
            dp[at, :] = dp[at, :] * coef - ps[at, :] * valid * cb
        return 0

    lax.fori_loop(0, nw // 4, make, 0)

    gss, grs = r["gsem"]
    def place(d):
        return lax.rem(me_t + far_first(d, tiles), tiles)

    def points_copy(d):
        t = place(d)
        return remote(gout.at[t], gp.at[me_t], gss.at[d], grs.at[d], "tile", t)

    def put_points(t, at, rows):
        gout[t, :, at] = rows

    def one_bucket(d, _):
        point_bucket(place(d), slots, feats, w_vfe, b_vfe, dp, got, put_points, gw, gb)

        @pl.when(d < tiles - 1)
        def _():
            points_copy(d).start()

        for at, action in ((2, lay0.step2), (3, early.middle), (4, lay0.step3), (6, lay0.step4)):
            pl.when(d == at)(action)
        return 0

    lax.fori_loop(0, tiles, one_bucket, 0)
    gp_own = pltpu.make_async_copy(gout.at[me_t], gp.at[me_t], own.at[2])
    gp_own.start()

    late.start(
        jnp.concatenate(
            [
                gw[...], jnp.sum(gb[...], axis=0, keepdims=True), local_dot * scale,
                jnp.zeros((6, D), f32),
            ],
            axis=0,
        )
    )
    small[0:VFE_ROW, :] = early.total()
    late.middle()
    lay1.step5()
    lay0.step5()
    po_copy().wait()
    po_own.wait()
    gp_own.wait()
    for d in range(tiles - 1):
        points_copy(d).wait()
    small[VFE_ROW : VFE_ROW + 24, :] = late.total()


def finish_kernel(po, gp, full0, full1, small, *outs):
    (
        o_po, o_gp, g_w_vfe, g_b_vfe, g_gain, g_qkv, g_bqv, g_out, g_bout, g_ga, g_ba, g_in, g_bin,
        g_back, g_bback, g_gf, g_bf,
    ) = outs
    o_po[0] = po[...]
    tiles, _, bucket = gp.shape
    for t in range(tiles):
        o_gp[0, :, t * bucket : (t + 1) * bucket] = gp[t]
    g_w_vfe[...] = small[VFE_ROW : VFE_ROW + 16, :]
    g_b_vfe[...] = small[VFE_ROW + 16 : VFE_ROW + 17, :]
    g_gain[...] = small[VFE_ROW + 17 : VFE_ROW + 18, :]
    for l, full in enumerate((full0, full1)):
        one = slice(l, l + 1)

        def row(i):
            return small[16 * l + i : 16 * l + i + 1, :]

        g_bqv[one, 0:D] = row(0)
        g_bqv[one, D:] = row(2)
        g_bout[one, :] = row(3)
        g_ga[one, :] = row(4)
        g_ba[one, :] = row(5)
        g_bin[one, 0:D] = row(6)
        g_bin[one, D:] = row(7)
        g_bback[one, :] = row(8)
        g_gf[one, :] = row(9)
        g_bf[one, :] = row(10)
        per = full.shape[1]

        def block(i):
            r = i * D
            return full[r // per, r % per : r % per + D, :].astype(f32)

        for i in range(3):
            g_qkv[l, :, i * D : (i + 1) * D] = block(i)
        g_out[l] = block(3)
        for i in range(2):
            g_in[l, :, i * D : (i + 1) * D] = block(4 + i)
            g_back[l, i * D : (i + 1) * D, :] = block(6 + i)


def shape(s, t):
    return jax.ShapeDtypeStruct(s, t)


def call(kernel, out_shape, n_smem, n_in, scratch, *args):
    return pl.pallas_call(
        kernel,
        out_shape=out_shape,
        in_specs=[SMEM] * n_smem + [VMEM] * (n_in - n_smem),
        out_specs=jax.tree.map(lambda _: VMEM, out_shape),
        scratch_shapes=scratch,
        compiler_params=pltpu.CompilerParams(vmem_limit_bytes=VMEM_LIMIT),
    )(*args)


def passed_along(value, axis, steps):
    count = lax.axis_size(axis)
    return lax.ppermute(value, axis, [(i, (i + steps) % count) for i in range(count)])


def unpack(acc):
    a_qkv, a_out, a_in, a_back, a_vec = acc
    b_all = a_qkv[D]
    vec = jnp.sum(a_vec, axis=2)
    return (
        a_qkv[0:D],
        jnp.concatenate([b_all[0:D], b_all[2 * D :]]),
        a_out[0:D],
        a_out[D],
        vec[2],
        vec[3],
        a_in[0:D],
        a_in[D],
        a_back[0:FF],
        a_back[FF],
        vec[0],
        vec[1],
    )


def fused(frames, tiles, *args):
    point_feats, point_slot, bucket_len, window_len, w_vfe, b_vfe, gain_vfe = args[:7]
    weights, cotangent = args[7:19], args[19]
    _, pf, points = point_feats.shape
    bucket = points // tiles
    nw = window_len.shape[1]
    n = nw * WSLOT
    any_space = pl.BlockSpec(memory_space=pl.ANY)
    dma = pltpu.SemaphoreType.DMA
    rows = slot_rows(bucket)
    got_feats, got_slots, next_len = pl.pallas_call(
        functools.partial(exchange_kernel, tiles, n),
        out_shape=(
            shape((tiles, pf, bucket), bf16), shape((tiles, rows, D), jnp.int32),
            shape((8, D), jnp.int32),
        ),
        in_specs=[SMEM, SMEM, VMEM, VMEM],
        out_specs=(VMEM, VMEM, VMEM),
        scratch_shapes=[
            pltpu.VMEM((tiles, pf, bucket), bf16), pltpu.VMEM((tiles, rows, D), jnp.int32),
            pltpu.VMEM((8, D), jnp.int32),
            dma((tiles - 1,)), dma((tiles - 1,)), dma((tiles - 1,)), dma((tiles - 1,)),
            dma((1,)), dma((1,)),
        ],
        compiler_params=pltpu.CompilerParams(
            vmem_limit_bytes=VMEM_LIMIT, collective_id=0, has_side_effects=True
        ),
    )(bucket_len, window_len, point_slot, point_feats)
    got_slots = got_slots.reshape(-1)
    b_row = b_vfe[None, :]
    ps, stat = call(
        functools.partial(scatter_kernel, nw),
        (shape((n, D), f32), shape((8, D), f32)),
        2, 5,
        [pltpu.VMEM((bucket, D), f32)] + [pltpu.VMEM((n + 128, D), f32)] * NACC,
        got_slots, window_len, got_feats, w_vfe, b_row,
    )
    spec = main_scratch(frames, tiles, nw, pf, bucket)
    per_f = Reducer.ROWS // frames
    po, gp, full0, full1, small = pl.pallas_call(
        functools.partial(main_kernel, frames, tiles, nw, GROUP, spec),
        out_shape=(
            shape((n, D), bf16), shape((tiles, pf, bucket), bf16), shape((frames, per_f, D), bf16),
            shape((frames, per_f, D), bf16), shape((EXTRA, D), f32),
        ),
        in_specs=[SMEM] * 3 + [any_space] + [VMEM] * 18,
        out_specs=(any_space, any_space, VMEM, VMEM, VMEM),
        scratch_shapes=[entry for entries in spec.values() for entry in entries],
        compiler_params=pltpu.CompilerParams(
            vmem_limit_bytes=MAIN_LIMIT, collective_id=1, has_side_effects=True
        ),
    )(
        got_slots, window_len, next_len, cotangent, stat, ps, got_feats, w_vfe, b_row,
        gain_vfe[None, :], *weights,
    )
    out_shape = (
        shape((1, n, D), bf16), shape((1, pf, points), bf16),
        shape((pf, D), f32), shape((1, D), f32), shape((1, D), f32),
        shape((2, D, 3 * D), f32), shape((2, 2 * D), f32), shape((2, D, D), f32), shape((2, D), f32),
        shape((2, D), f32), shape((2, D), f32), shape((2, D, FF), f32), shape((2, FF), f32),
        shape((2, FF, D), f32), shape((2, D), f32), shape((2, D), f32), shape((2, D), f32),
    )
    outs = pl.pallas_call(
        finish_kernel,
        out_shape=out_shape,
        in_specs=[VMEM] * 5,
        out_specs=(VMEM,) * 17,
        compiler_params=pltpu.CompilerParams(vmem_limit_bytes=VMEM_LIMIT),
    )(po, gp, full0, full1, small)
    return (*outs[:3], outs[3][0], outs[4][0], *outs[5:])


def stepwise(
    tiles, point_feats, point_slot, bucket_len, window_len, w_vfe, b_vfe, gain_vfe, *rest
):
    weights, cotangent = rest[:12], rest[12]
    feats = point_feats[0]
    pf, points = feats.shape
    bucket = points // tiles
    nw = window_len.shape[1]
    n = nw * WSLOT
    half = WSLOT // 2
    live = jnp.arange(bucket, dtype=jnp.int32)[None, :] < bucket_len[0][:, None]
    target = jnp.where(live, point_slot[0].reshape(tiles, bucket), n)
    a2a = functools.partial(lax.all_to_all, axis_name="tile", split_axis=0, concat_axis=0, tiled=True)
    got_feats = a2a(feats.reshape(pf, tiles, bucket).transpose(1, 0, 2))
    target = target[:, : bucket // 2] + target[:, bucket // 2 :] * 65536
    got_slots = a2a(target).reshape(-1)
    lens = jnp.concatenate([window_len[0], passed_along(window_len[0, 0:1], "tile", -1)])
    b_row = b_vfe[None, :]
    acc_rows = n + 128
    ps, stat = call(
        functools.partial(scatter_kernel, nw),
        (shape((n, D), f32), shape((8, D), f32)),
        2, 5,
        [pltpu.VMEM((bucket, D), f32)] + [pltpu.VMEM((acc_rows, D), f32)] * NACC,
        got_slots, window_len, got_feats, w_vfe, b_row,
    )
    sums = lax.psum(stat[0:2], "tile")
    count = sums[1]
    scale = lax.rsqrt(sums[0] / count + EPS)
    coef = (scale * gain_vfe)[None, :]
    fo = call(
        functools.partial(first_forward_kernel, nw, GROUP),
        shape((nw, D, WSLOT), f32), 1, 15, layer_scratch(),
        lens, ps, coef, *weights,
    )
    rim = passed_along(fo[0].astype(bf16), "tile", -1)
    cot = cotangent[0]
    rim_cot = passed_along(cot[:half], "tile", -1)
    acc_out = tuple(shape(a, f32) for a in ACC_SHAPES)
    second = call(
        functools.partial(second_kernel, nw, GROUP),
        (shape((n, D), bf16), shape((nw, D, WSLOT), f32)) + acc_out,
        1, 17,
        layer_scratch() + [pltpu.VMEM((nw + 1, D, WSLOT), f32), pltpu.VMEM((n, D), bf16)],
        lens, fo, rim, cot, rim_cot, *weights,
    )
    view, gv = second[0], second[1]
    back_rim = passed_along(view[n - half :], "tile", 1)
    pillar_out = jnp.concatenate([back_rim, view[: n - half]], axis=0)[None]
    back = passed_along(gv[nw - 1].astype(bf16), "tile", 1)
    first = call(
        functools.partial(first_backward_kernel, nw, GROUP),
        (shape((n, D), f32),) + acc_out,
        1, 17,
        layer_scratch() + [pltpu.VMEM((nw + 1, D, WSLOT), f32)],
        lens, ps, coef, gv, back, *weights,
    )
    d_enc = first[0]
    local_dot = jnp.sum(d_enc * ps, axis=0)
    dots = lax.psum(local_dot, "tile")
    cb = (gain_vfe * scale**3 * dots / count)[None, :]
    out, gw, gb = call(
        functools.partial(gather_kernel, nw),
        (shape((tiles, pf, bucket), bf16), shape((pf, D), f32), shape((8, D), f32)),
        2, 9,
        [pltpu.VMEM((acc_rows, D), f32), pltpu.VMEM((bucket, D), f32)],
        got_slots, window_len, got_feats, w_vfe, b_row, d_enc, ps, coef, cb,
    )
    grad_points = a2a(out).transpose(1, 0, 2).reshape(pf, points)[None]
    g_zero, g_one, g_pts = lax.psum(
        (
            unpack(first[1:]), unpack(second[2:]),
            (gw, jnp.sum(gb, axis=0), local_dot * scale),
        ),
        ("frame", "tile"),
    )
    layer = [jnp.stack([a, b]) for a, b in zip(g_zero, g_one)]
    return (pillar_out, grad_points, *g_pts, *layer)


def local(*args):
    frames, tiles = lax.axis_size("frame"), lax.axis_size("tile")
    bucket = args[0].shape[2] // tiles
    even = Reducer.ROWS % (frames * tiles * 16) == 0 and EXTRA % (tiles * 8) == 0
    if even and bucket % (2 * D) == 0:
        return fused(frames, tiles, *args)
    return stepwise(tiles, *args)


def solution(mesh):
    rep = P()
    rows = P("frame", "tile")
    return jax.shard_map(
        local,
        mesh=mesh,
        in_specs=(P("frame", None, "tile"), rows, rows, rows)
        + (rep,) * 15
        + (P("frame", "tile", None),),
        out_specs=(P("frame", "tile", None), P("frame", None, "tile")) + (rep,) * 15,
        check_vma=False,
    )
```
